32 devices in a mesh: groups: 2 (over x), wide: 8 (over z, y), hid: 2 (over core).
Axes of the slice: x: 2, y: 2, z: 4, core: 2. Of those that a mesh axis runs over, the one named last changes fastest.
Arguments:
- tokens: bfloat16 [4096, 7168], P(('groups', 'hid'), 'wide'), parts along dimension 0, may hold values from -6 to 6
- expert_ids: int32 [4096, 2], P('groups'), parts along dimension 0, may hold values from 0 to 15, all different within a row; in each aligned block of 2048 rows (0 to 2047, 2048 to 4095, ...) at most 384 rows name the same one
- gate_scale: float32 [4096, 2], P('groups'), parts along dimension 0, may hold values from 0.2 to 1
- gate_weight: bfloat16 [16, 7168, 1024], P(None, 'wide', 'hid'), may hold values from -0.0625 to 0.0625
- up_weight: bfloat16 [16, 7168, 1024], P(None, 'wide', 'hid'), may hold values from -0.0625 to 0.0625
- down_weight: bfloat16 [16, 1024, 7168], P(None, 'hid', 'wide'), may hold values from -0.1875 to 0.1875
Outputs:
- layer_output: bfloat16 [4096, 7168], P(('groups', 'hid'), 'wide'), parts along dimension 0
The draws below stay inside these ranges and needn't reach their ends.
There are 2 independent parts, one for each index of `groups`. The reference program is written for one: setup_inputs(seed, part) draws one part's arguments, and reference() takes and returns one part's arrays. A program takes and returns all parts, laid end to end along the dimension named above; an argument that names none is the same for every part. Nothing has to cross between parts.
Inputs may be any that keep to these rules, and one draw needn't show every extreme that they name: `expert_ids`: the 2 entries of a token are different experts. In each part no expert is named by more than 384 tokens, a bound that some block reaches; every expert is named by some token.
All inputs are finite; a program needn't handle non-finite values.
Results may differ from the reference program's by a relative error of at most 0.02.
Values may be sent and summed in bfloat16 or wider, within the bound.
A program may use at most 192 MiB of HBM per device.

```python
import math
import jax
import jax.numpy as jnp
import numpy as np
from jax import lax

D = 7168
H = 1024
EXPERTS = 16
SLAB_K = 2
TOKENS = 2048
CAP = 384
N_WIDE = 8


def steps_of(own_key, dims, pieces, smallest, largest):
    level, own = 1.0, jax.random.fold_in(own_key, 6)
    for position, parts in pieces:
        steps = jnp.exp(jax.random.uniform(jax.random.fold_in(own, position), (parts,), jnp.float32, smallest / len(pieces), largest / len(pieces)))
        level = level * jnp.repeat(steps, dims[position] // parts).reshape([-1 if axis == position else 1 for axis in range(len(dims))])
    return level


def routed_block(rng, own, number, rows, count, top, limit, slope):
    ranking = jax.random.permutation(rng, count)
    heavy_load, ordinary = shares(count, rows * top, limit, slope, True), shares(count, rows * top, limit, slope, False)
    places = jnp.arange(count)

    def named(tallies, rotation):
        used = int((tallies > 0).sum())
        fixed = max(1, used // 4)
        shifted = fixed + (places - fixed + rotation * (used - fixed)) % max(1, count - fixed)
        return jnp.zeros((count,), jnp.int32).at[ranking[jnp.where(places < fixed, places, shifted)]].set(jnp.asarray(tallies, jnp.int32))

    tallies = jnp.where(number % 4 == 0, named(heavy_load, number // 4), named(ordinary, number - number // 4 - 1))
    mixed = jax.random.permutation(jax.random.fold_in(own, 3), count)
    giver, sink = mixed[0:count // 2 * 2:2], mixed[1:count // 2 * 2:2]
    room = jnp.minimum(tallies[giver] - 1, limit - tallies[sink]) // 2
    room = jnp.where((giver == ranking[0]) | (sink == ranking[0]) | (tallies[sink] == 0), 0, jnp.maximum(room, 0))
    shifted = jax.random.randint(jax.random.fold_in(own, 4), (count // 2,), 0, 1 << 20) % (room + 1)
    tallies = tallies.at[giver].add(-shifted).at[sink].add(shifted)
    items = jnp.searchsorted(jnp.cumsum(tallies), jnp.arange(rows * top), side="right").astype(jnp.int32)
    grid = items.reshape(top, rows).T
    grid = grid[jax.random.permutation(jax.random.fold_in(own, 1), rows)]
    rotation = jax.random.randint(jax.random.fold_in(own, 2), (rows, 1), 0, top)
    return jnp.take_along_axis(grid, (jnp.arange(top)[None, :] + rotation) % top, axis=1)


def shares(number_of, total, limit, lean, full):
    loads = [(1 << 20) // math.isqrt(rank ** lean) + 1 for rank in range(1, number_of + 1)]
    largest = limit if full else min(limit, max(-(-total // number_of), total * loads[0] // sum(loads)))
    least = 1 if total - largest >= number_of - 1 else 0
    counts, spare = [largest] + [least] * (number_of - 1), total - largest - least * (number_of - 1)
    while spare > 0:
        free = [i for i in range(1, number_of) if counts[i] < largest] or [i for i in range(1, number_of) if counts[i] < limit]
        whole, remaining = sum([loads[i] for i in free]), spare
        for i in free:
            addition = min(limit - counts[i], max(1, remaining * loads[i] // whole), spare)
            counts[i] = counts[i] + addition
            spare = spare - addition
    return np.array(counts)


def bell_draw(own_key, extent, scale, bound, cuts=(), held_as=jnp.bfloat16):
    drawn = jax.random.normal(own_key, extent, jnp.float32) * scale
    if len(cuts) > 0:
        drawn = steps_of(own_key, extent, cuts, -0.22, 0.18) * drawn
    return jnp.clip(drawn, min=-bound, max=bound).astype(held_as)


def setup_inputs(seed: int = 0, part: int = 0) -> dict:
    arg_keys = jax.random.split(jax.random.key(seed), 7)
    part_keys = jax.random.split(jax.random.fold_in(arg_keys[6], part), 7)
    tokens = bell_draw(part_keys[0], (TOKENS, D), 1.0, 6.0, ((0, 2), (1, 8)))
    expert_ids_keys = jax.random.split(jax.random.fold_in(part_keys[1], 1), TOKENS // TOKENS)
    expert_ids_turns = jax.random.permutation(jax.random.fold_in(part_keys[1], 3), TOKENS // TOKENS)
    expert_ids = jax.vmap(lambda own, number: routed_block(jax.random.fold_in(part_keys[1], 2), own, number, TOKENS, EXPERTS, SLAB_K, CAP, 2))(expert_ids_keys, expert_ids_turns).reshape((TOKENS, SLAB_K))
    gate_scale = jnp.clip(jax.random.uniform(part_keys[2], (TOKENS, SLAB_K), jnp.float32, 0.2, 1.0), 0.2, 1.0)
    gate_weight = bell_draw(arg_keys[3], (EXPERTS, D, H), D ** -0.5, 0.0625, ((1, 8), (2, 2)))
    up_weight = bell_draw(arg_keys[4], (EXPERTS, D, H), D ** -0.5, 0.0625, ((1, 8), (2, 2)))
    down_weight = bell_draw(arg_keys[5], (EXPERTS, H, D), H ** -0.5, 0.1875, ((1, 2), (2, 8)))
    return {"tokens": tokens, "expert_ids": expert_ids, "gate_scale": gate_scale, "gate_weight": gate_weight, "up_weight": up_weight, "down_weight": down_weight}


def slot_rank_of(expert_ids, experts):
    flat_ids = expert_ids.reshape(-1).astype(jnp.int32)
    labels = jnp.arange(experts, dtype=jnp.int32)
    onehot = (flat_ids[:, None] == labels[None, :]).astype(jnp.int32)
    earlier = (jnp.cumsum(onehot, axis=0) - onehot).astype(jnp.int32)
    slot_rank = jnp.sum(earlier * onehot, axis=1).astype(jnp.int32)
    return flat_ids, slot_rank


def reference(tokens, expert_ids, gate_scale, gate_weight, up_weight, down_weight):
    flat_ids, slot_rank = slot_rank_of(expert_ids, EXPERTS)
    row_index = (flat_ids * CAP + slot_rank).astype(jnp.int32)
    owner_token = (jnp.arange(TOKENS * SLAB_K, dtype=jnp.int32) // SLAB_K).astype(jnp.int32)
    source = jnp.zeros((EXPERTS * CAP,), jnp.int32).at[row_index].set(owner_token)
    gathered = tokens[source].reshape(EXPERTS, CAP, D)
    slice_width = D // N_WIDE

    def sliced(expert_block, weight):
        left_side = expert_block.reshape(CAP, N_WIDE, slice_width).astype(jnp.float32)
        right_side = weight.reshape(N_WIDE, slice_width, H).astype(jnp.float32)
        partial_sums = jnp.einsum("cnd,ndh->nch", left_side, right_side)
        rounded = lax.optimization_barrier(partial_sums.astype(jnp.bfloat16))
        return jnp.sum(rounded.astype(jnp.float32), axis=0)

    def expert_rows(operands):
        expert_block, w_gate, w_up, w_down = operands
        hidden = (jax.nn.silu(sliced(expert_block, w_gate)) * sliced(expert_block, w_up)).astype(jnp.bfloat16)
        return jnp.dot(hidden, w_down, preferred_element_type=jnp.float32)

    outputs = lax.map(expert_rows, (gathered, gate_weight, up_weight, down_weight)).reshape(EXPERTS * CAP, D)
    picked = outputs[row_index].reshape(TOKENS, SLAB_K, D)
    combined = jnp.sum(gate_scale[:, :, None].astype(jnp.float32) * picked, axis=1)
    return combined.astype(jnp.bfloat16)
```

```python
import functools

import jax
import jax.numpy as jnp
from jax import lax
from jax.experimental import pallas as pl
from jax.experimental.pallas import tpu as pltpu
from jax.sharding import PartitionSpec as P

row_align = 16
lane_width = 128
gather_rows = 256
vmem_bytes = 60 * 1024 * 1024


def round_up(value, unit):
    return (value + unit - 1) // unit * unit


def routing_tables(expert_ids, experts):
    flat_ids = expert_ids.reshape(-1)
    labels = jnp.arange(experts, dtype=jnp.int32)
    onehot = (labels[:, None] == flat_ids[None, :]).astype(jnp.int32)
    running = jnp.cumsum(onehot, axis=1)
    counts = running[:, -1]
    padded = (counts + row_align - 1) // row_align * row_align
    starts = jnp.sum(jnp.where(labels[None, :] < labels[:, None], padded[None, :], 0), axis=1)
    place = jnp.sum(onehot * (running - 1 + starts[:, None]), axis=0)
    return place.reshape(expert_ids.shape), jnp.concatenate([starts, counts]).astype(jnp.int32)


def up_kernel(experts, real_rows, rows, block, table, place, tokens, gate, up, out, gathered):
    expert = pl.program_id(0)

    @pl.when(expert == 0)
    def _():
        tail = gathered.shape[0] - rows
        gathered[rows:, :] = jnp.zeros((tail, gathered.shape[1]), gathered.dtype)
        rest = out.shape[1] - real_rows
        out[:, real_rows:, :] = jnp.zeros((out.shape[0], rest, out.shape[2]), out.dtype)
        first, second = place[0:1, :], place[1:2, :]

        def gather(step, carry):
            base = pl.multiple_of(step * gather_rows, gather_rows)
            ids = lax.broadcasted_iota(jnp.int32, (gather_rows, tokens.shape[0]), 0) + base
            chosen = jnp.where((ids == first) | (ids == second), 1.0, 0.0).astype(jnp.bfloat16)
            picked = jnp.dot(chosen, tokens[...], preferred_element_type=jnp.float32)
            gathered[pl.ds(base, gather_rows), :] = picked.astype(jnp.bfloat16)
            return carry

        lax.fori_loop(0, rows // gather_rows, gather, 0)

    start, count = table[expert], table[experts + expert]

    def multiply(step, carry):
        base = pl.multiple_of(start + step * block, row_align)
        part = gathered[pl.ds(base, block), :]
        gates = jnp.dot(part, gate[0], preferred_element_type=jnp.float32).astype(jnp.bfloat16)
        ups = jnp.dot(part, up[0], preferred_element_type=jnp.float32).astype(jnp.bfloat16)
        for s in range(out.shape[0]):
            cut = slice(s * lane_width, (s + 1) * lane_width)
            out[s, pl.ds(base, block), 0:lane_width] = gates[:, cut]
            out[s, pl.ds(base, block), lane_width:] = ups[:, cut]
        return carry

    lax.fori_loop(0, (count + block - 1) // block, multiply, 0)


def exchange_kernel(n, rows, partial, result, own, paired, summed, hidden, *sems):
    own_sem, y_send, y_recv, z_send, z_recv, g_send, g_recv, h_send, h_recv, out_sem = sems
    slices = own.shape[0]
    depth = n // 2
    chunk = rows // n
    half = rows // 2
    me = lax.axis_index("wide")
    y, z = lax.rem(me, 2), lax.div(me, 2)
    y_peer = {"wide": me + 1 - 2 * y}
    ahead = [{"wide": lax.rem(z + j, depth) * 2 + y} for j in range(depth)]
    mesh_type = pl.DeviceIdType.MESH

    own_base = pl.multiple_of(y * half, row_align)
    peer_base = pl.multiple_of((1 - y) * half, row_align)
    my_rows = pl.ds(pl.multiple_of(y * half + z * chunk, row_align), chunk)
    my_part = pl.ds(pl.multiple_of(z * chunk, row_align), chunk)

    def own_copy(s):
        return pltpu.make_async_copy(
            partial.at[s, pl.ds(own_base, half)], own.at[s], own_sem.at[s]
        )

    def y_copy(s):
        return pltpu.make_async_remote_copy(
            partial.at[s, pl.ds(peer_base, half)], paired.at[s],
            y_send.at[s], y_recv.at[s], y_peer, mesh_type,
        )

    def z_copy(s, j):
        part = pl.ds(pl.multiple_of(lax.rem(z + j, depth) * chunk, row_align), chunk)
        return pltpu.make_async_remote_copy(
            own.at[s, part], summed.at[s, j - 1],
            z_send.at[s, j - 1], z_recv.at[s, j - 1], ahead[j], mesh_type,
        )

    def g_copy(s, j):
        return pltpu.make_async_remote_copy(
            hidden.at[s, my_rows], hidden.at[s, my_rows],
            g_send.at[s, j - 1], g_recv.at[s, j - 1], ahead[j], mesh_type,
        )

    def h_copy(s):
        return pltpu.make_async_remote_copy(
            hidden.at[s, pl.ds(own_base, half)], hidden.at[s, pl.ds(own_base, half)],
            h_send.at[s], h_recv.at[s], y_peer, mesh_type,
        )

    def out_copy(s):
        return pltpu.make_async_copy(
            hidden.at[s], result.at[s, pl.ds(0, rows)], out_sem.at[s]
        )

    barrier = pltpu.get_barrier_semaphore()
    for peer in [y_peer] + ahead[1:]:
        pl.semaphore_signal(barrier, inc=1, device_id=peer, device_id_type=mesh_type)
    for s in range(slices):
        own_copy(s).start()
    pl.semaphore_wait(barrier, depth)
    for s in range(min(2, slices)):
        y_copy(s).start()
    far_first = sorted(range(1, depth), key=lambda j: -min(j, depth - j))

    for step in range(slices + 2):
        s = step
        if s < slices:
            own_copy(s).wait()
            y_copy(s).wait_recv()

            def add(j, carry, s=s):
                part = pl.ds(pl.multiple_of(j * chunk, row_align), chunk)
                own[s, part] = (
                    own[s, part].astype(jnp.float32) + paired[s, part].astype(jnp.float32)
                ).astype(jnp.bfloat16)
                return carry

            lax.fori_loop(0, depth, add, 0)
            for j in far_first:
                z_copy(s, j).start()
            if s + 2 < slices:
                y_copy(s + 2).start()
        s = step - 1
        if 0 <= s < slices:
            total = own[s, my_part].astype(jnp.float32)
            for j in far_first:
                z_copy(s, j).wait_recv()
            for j in range(1, depth):
                total = total + summed[s, j - 1].astype(jnp.float32)
            gates, ups = total[:, :lane_width], total[:, lane_width:]
            hidden[s, my_rows] = (gates / (1.0 + jnp.exp(-gates)) * ups).astype(jnp.bfloat16)
            for j in far_first:
                g_copy(s, j).start()
        s = step - 2
        if 0 <= s < slices:
            for j in far_first:
                g_copy(s, j).wait_recv()
            h_copy(s).start()
    for s in range(slices):
        h_copy(s).wait_recv()
        out_copy(s).start()
    for s in range(slices):
        y_copy(s).wait_send()
        for j in range(1, depth):
            z_copy(s, j).wait_send()
            g_copy(s, j).wait_send()
        h_copy(s).wait_send()
        out_copy(s).wait()


def down_kernel(experts, real_rows, rows, block, table, place, scale, hidden, weight, out, held):
    expert = pl.program_id(0)

    @pl.when(expert == 0)
    def _():
        rest = held.shape[0] - real_rows
        held[real_rows:, :] = jnp.zeros((rest, held.shape[1]), held.dtype)

    start, count = table[expert], table[experts + expert]

    def multiply(step, carry):
        base = pl.multiple_of(start + step * block, row_align)
        part = jnp.concatenate(
            [hidden[s, pl.ds(base, block), :] for s in range(hidden.shape[0])], axis=1
        )
        product = jnp.dot(part, weight[0], preferred_element_type=jnp.float32)
        held[pl.ds(base, block), :] = product.astype(jnp.bfloat16)
        return carry

    lax.fori_loop(0, (count + block - 1) // block, multiply, 0)

    @pl.when(expert == experts - 1)
    def _():
        def combine(step, carry):
            base = pl.multiple_of(step * gather_rows, gather_rows)
            span = pl.ds(base, gather_rows)
            ids = lax.broadcasted_iota(jnp.int32, (gather_rows, rows), 1)
            places, scales = place[span, :], scale[span, :]
            mixed = jnp.where(
                ids == places[:, 0:1], scales[:, 0:1],
                jnp.where(ids == places[:, 1:2], scales[:, 1:2], 0.0),
            ).astype(jnp.bfloat16)
            total = jnp.dot(mixed, held[0:rows, :], preferred_element_type=jnp.float32)
            out[span, :] = total.astype(jnp.bfloat16)
            return carry

        lax.fori_loop(0, out.shape[0] // gather_rows, combine, 0)


def whole_block(shape):
    return pl.BlockSpec(
        shape, lambda e, table: (0,) * len(shape), pipeline_mode=pl.Buffered(1)
    )


def body(n, tokens, expert_ids, gate_scale, gate_weight, up_weight, down_weight):
    token_total, slot_count = expert_ids.shape
    experts, width, half_hidden = gate_weight.shape
    slices = half_hidden // lane_width
    depth = n // 2
    real_rows = token_total * slot_count
    capacity = round_up(real_rows * 3 // (2 * experts), 2 * row_align)
    block = capacity // 2
    rows = round_up(real_rows + row_align * experts, max(n * row_align, gather_rows))
    chunk = rows // n
    all_rows = rows + capacity
    bf16 = jnp.bfloat16

    place, table = routing_tables(expert_ids, experts)
    features = lax.all_gather(tokens, "hid", axis=0, tiled=True)

    partial = pl.pallas_call(
        functools.partial(up_kernel, experts, real_rows, rows, block),
        out_shape=jax.ShapeDtypeStruct((slices, all_rows, 2 * lane_width), bf16),
        grid_spec=pltpu.PrefetchScalarGridSpec(
            num_scalar_prefetch=1,
            grid=(experts,),
            in_specs=[
                whole_block((slot_count, token_total)),
                whole_block((token_total, width)),
                pl.BlockSpec((1, width, half_hidden), lambda e, table: (e, 0, 0)),
                pl.BlockSpec((1, width, half_hidden), lambda e, table: (e, 0, 0)),
            ],
            out_specs=whole_block((slices, all_rows, 2 * lane_width)),
            scratch_shapes=[pltpu.VMEM((all_rows, width), bf16)],
        ),
        compiler_params=pltpu.CompilerParams(vmem_limit_bytes=vmem_bytes),
    )(table, place.T, features, gate_weight, up_weight)

    dma = pltpu.SemaphoreType.DMA
    hidden = pl.pallas_call(
        functools.partial(exchange_kernel, n, rows),
        out_shape=jax.ShapeDtypeStruct((slices, all_rows, lane_width), bf16),
        in_specs=[pl.BlockSpec(memory_space=pl.ANY)],
        out_specs=pl.BlockSpec(memory_space=pl.ANY),
        scratch_shapes=[
            pltpu.VMEM((slices, rows // 2, 2 * lane_width), bf16),
            pltpu.VMEM((slices, rows // 2, 2 * lane_width), bf16),
            pltpu.VMEM((slices, depth - 1, chunk, 2 * lane_width), bf16),
            pltpu.VMEM((slices, rows, lane_width), bf16),
            dma((slices,)),
            dma((slices,)),
            dma((slices,)),
            dma((slices, depth - 1)),
            dma((slices, depth - 1)),
            dma((slices, depth - 1)),
            dma((slices, depth - 1)),
            dma((slices,)),
            dma((slices,)),
            dma((slices,)),
        ],
        compiler_params=pltpu.CompilerParams(
            collective_id=0, has_side_effects=True, vmem_limit_bytes=vmem_bytes
        ),
    )(partial)

    combined = pl.pallas_call(
        functools.partial(down_kernel, experts, real_rows, rows, block),
        out_shape=jax.ShapeDtypeStruct((token_total, width), bf16),
        grid_spec=pltpu.PrefetchScalarGridSpec(
            num_scalar_prefetch=1,
            grid=(experts,),
            in_specs=[
                whole_block((token_total, slot_count)),
                whole_block((token_total, slot_count)),
                whole_block((slices, all_rows, lane_width)),
                pl.BlockSpec((1, half_hidden, width), lambda e, table: (e, 0, 0)),
            ],
            out_specs=whole_block((token_total, width)),
            scratch_shapes=[pltpu.VMEM((all_rows, width), bf16)],
        ),
        compiler_params=pltpu.CompilerParams(vmem_limit_bytes=vmem_bytes),
    )(table, place, gate_scale, hidden, down_weight)
    return lax.psum_scatter(combined, "hid", scatter_dimension=0, tiled=True)


def solution(mesh):
    placed = (
        P(("groups", "hid"), "wide"),
        P("groups", None),
        P("groups", None),
        P(None, "wide", "hid"),
        P(None, "wide", "hid"),
        P(None, "hid", "wide"),
    )
    return jax.shard_map(
        functools.partial(body, mesh.shape["wide"]),
        mesh=mesh,
        in_specs=placed,
        out_specs=P(("groups", "hid"), "wide"),
        check_vma=False,
    )
```

```python
import functools

import jax
import jax.numpy as jnp
from jax import lax
from jax.experimental import pallas as pl
from jax.experimental.pallas import tpu as pltpu
from jax.sharding import PartitionSpec as P

row_align = 16
lane_width = 128
row_unit = 256
combine_step = 512
y_window = 3
vmem_bytes = 60 * 1024 * 1024


def round_up(value, unit):
    return (value + unit - 1) // unit * unit


def routing_tables(expert_ids, experts):
    flat_ids = expert_ids.reshape(-1)
    labels = jnp.arange(experts, dtype=jnp.int32)
    onehot = (labels[:, None] == flat_ids[None, :]).astype(jnp.int32)
    running = jnp.cumsum(onehot, axis=1)
    counts = running[:, -1]
    padded = (counts + row_align - 1) // row_align * row_align
    starts = jnp.sum(jnp.where(labels[None, :] < labels[:, None], padded[None, :], 0), axis=1)
    place = jnp.sum(onehot * (running - 1 + starts[:, None]), axis=0)
    return place.reshape(expert_ids.shape), jnp.concatenate([starts, counts]).astype(jnp.int32)


def up_kernel(experts, real_rows, rows, step_rows, block, table, place, mine, peer, gate, up, out, gathered):
    expert = pl.program_id(0)
    half = mine.shape[0]

    @pl.when(expert == 0)
    def _():
        tail = gathered.shape[0] - rows
        gathered[rows:, :] = jnp.zeros((tail, gathered.shape[1]), gathered.dtype)
        rest = out.shape[1] - real_rows
        out[:, real_rows:, :] = jnp.zeros((out.shape[0], rest, out.shape[2]), out.dtype)
        first, second = place[0:1, :], place[1:2, :]

        def gather(step, carry):
            base = pl.multiple_of(step * step_rows, row_align)
            ids = lax.broadcasted_iota(jnp.int32, (step_rows, 2 * half), 0) + base
            chosen = jnp.where((ids == first) | (ids == second), 1.0, 0.0).astype(jnp.bfloat16)
            picked = jnp.dot(chosen[:, :half], mine[...], preferred_element_type=jnp.float32)
            picked += jnp.dot(chosen[:, half:], peer[...], preferred_element_type=jnp.float32)
            gathered[pl.ds(base, step_rows), :] = picked.astype(jnp.bfloat16)
            return carry

        lax.fori_loop(0, rows // step_rows, gather, 0)

    base = pl.multiple_of(table[expert], row_align)
    part = gathered[pl.ds(base, block), :]
    gates = jnp.dot(part, gate[0], preferred_element_type=jnp.float32).astype(jnp.bfloat16)
    ups = jnp.dot(part, up[0], preferred_element_type=jnp.float32).astype(jnp.bfloat16)
    for s in range(out.shape[0]):
        cut = slice(s * lane_width, (s + 1) * lane_width)
        out[s, pl.ds(base, block), 0:lane_width] = gates[:, cut]
        out[s, pl.ds(base, block), lane_width:] = ups[:, cut]


def exchange_kernel(n, rows, partial, result, own, paired, summed, hidden, *sems):
    own_sem, y_send, y_recv, z_send, z_recv, g_send, g_recv, h_send, h_recv, out_sem = sems
    slices = own.shape[0]
    depth = n // 2
    chunk = rows // n
    half = rows // 2
    me = lax.axis_index("wide")
    y, z = lax.rem(me, 2), lax.div(me, 2)
    y_peer = {"wide": me + 1 - 2 * y}
    ahead = [{"wide": lax.rem(z + j, depth) * 2 + y} for j in range(depth)]
    mesh_type = pl.DeviceIdType.MESH

    def span(base, j):
        return pl.ds(pl.multiple_of(base + lax.rem(z + j, depth) * chunk, row_align), chunk)

    own_base = y * half
    peer_base = (1 - y) * half

    def own_copy(s):
        return pltpu.make_async_copy(
            partial.at[s, pl.ds(pl.multiple_of(own_base, row_align), half)],
            own.at[s], own_sem.at[s],
        )

    def y_copy(s, j):
        return pltpu.make_async_remote_copy(
            partial.at[s, span(peer_base, j)], paired.at[s, span(0, j)],
            y_send.at[s, j], y_recv.at[s, j], y_peer, mesh_type,
        )

    def z_copy(s, j):
        return pltpu.make_async_remote_copy(
            own.at[s, span(0, j)], summed.at[s, j - 1],
            z_send.at[s, j - 1], z_recv.at[s, j - 1], ahead[j], mesh_type,
        )

    def g_copy(s, j):
        return pltpu.make_async_remote_copy(
            hidden.at[s, span(own_base, 0)], hidden.at[s, span(own_base, 0)],
            g_send.at[s, j - 1], g_recv.at[s, j - 1], ahead[j], mesh_type,
        )

    def h_copy(s, j):
        rows_of = span(own_base, depth - j)
        return pltpu.make_async_remote_copy(
            hidden.at[s, rows_of], hidden.at[s, rows_of],
            h_send.at[s, j], h_recv.at[s, j], y_peer, mesh_type,
        )

    def out_copy(s):
        return pltpu.make_async_copy(
            hidden.at[s], result.at[s, pl.ds(0, rows)], out_sem.at[s]
        )

    barrier = pltpu.get_barrier_semaphore()
    for peer in [y_peer] + ahead[1:]:
        pl.semaphore_signal(barrier, inc=1, device_id=peer, device_id_type=mesh_type)
    for s in range(slices):
        own_copy(s).start()
    pl.semaphore_wait(barrier, depth)
    far_first = sorted(range(1, depth), key=lambda j: -min(j, depth - j))
    near_first = far_first[::-1]
    pieces = [(s, j) for s in range(slices) for j in far_first + [0]]
    for s, j in pieces[:y_window]:
        y_copy(s, j).start()

    def reduce(s):
        total = own[s, span(0, 0)].astype(jnp.float32)
        for j in near_first:
            z_copy(s, j).wait_recv()
        for j in near_first:
            total = total + summed[s, j - 1].astype(jnp.float32)
        gates, ups = total[:, :lane_width], total[:, lane_width:]
        hidden[s, span(own_base, 0)] = (gates / (1.0 + jnp.exp(-gates)) * ups).astype(jnp.bfloat16)
        for j in far_first:
            g_copy(s, j).start()
        h_copy(s, 0).start()

    def forward(s):
        for j in near_first:
            g_copy(s, j).wait_recv()
            h_copy(s, j).start()

    def finish(s):
        for j in range(depth):
            h_copy(s, j).wait_recv()
        out_copy(s).start()

    for step in range(slices + 3):
        if step < slices:
            own_copy(step).wait()
            for k in range(step * depth, (step + 1) * depth):
                s, j = pieces[k]
                y_copy(s, j).wait_recv()
                if k + y_window < len(pieces):
                    y_copy(*pieces[k + y_window]).start()
                part = span(0, j)
                own[s, part] = (
                    own[s, part].astype(jnp.float32) + paired[s, part].astype(jnp.float32)
                ).astype(jnp.bfloat16)
                if j > 0:
                    z_copy(s, j).start()
        if 0 <= step - 2 < slices:
            forward(step - 2)
        if 0 <= step - 1 < slices:
            reduce(step - 1)
        if 0 <= step - 3 < slices:
            finish(step - 3)
    for s in range(slices):
        for j in range(depth):
            y_copy(s, j).wait_send()
            h_copy(s, j).wait_send()
        for j in range(1, depth):
            z_copy(s, j).wait_send()
            g_copy(s, j).wait_send()
        out_copy(s).wait()


def combine_rows(rows, place, scale, held, out):
    def combine(step, carry):
        span = pl.ds(pl.multiple_of(step * combine_step, combine_step), combine_step)
        ids = lax.broadcasted_iota(jnp.int32, (combine_step, rows), 1)
        places, scales = place[span, :], scale[span, :]
        mixed = jnp.where(
            ids == places[:, 0:1], scales[:, 0:1],
            jnp.where(ids == places[:, 1:2], scales[:, 1:2], 0.0),
        ).astype(jnp.bfloat16)
        total = jnp.dot(mixed, held[0:rows, :], preferred_element_type=jnp.float32)
        out[span, :] = total.astype(out.dtype)
        return carry

    lax.fori_loop(0, out.shape[0] // combine_step, combine, 0)


def down_kernel(experts, real_rows, rows, block, table, place, scale, hidden, weight, out, held):
    expert = pl.program_id(0)

    @pl.when(expert == 0)
    def _():
        rest = held.shape[0] - real_rows
        held[real_rows:, :] = jnp.zeros((rest, held.shape[1]), held.dtype)

    base = pl.multiple_of(table[expert], row_align)
    part = jnp.concatenate(
        [hidden[s, pl.ds(base, block), :] for s in range(hidden.shape[0])], axis=1
    )
    product = jnp.dot(part, weight[0], preferred_element_type=jnp.float32)
    held[pl.ds(base, block), :] = product.astype(jnp.bfloat16)

    @pl.when(expert == experts - 1)
    def _():
        combine_rows(rows, place, scale, held, out)


def own_kernel(rows, place, scale, held, out):
    combine_rows(rows, place, scale, held, out)


def whole_block(shape):
    return pl.BlockSpec(
        shape, lambda e, table: (0,) * len(shape), pipeline_mode=pl.Buffered(1)
    )


def body(n, tokens, expert_ids, gate_scale, gate_weight, up_weight, down_weight):
    token_total, slot_count = expert_ids.shape
    experts, width, half_hidden = gate_weight.shape
    slices = half_hidden // lane_width
    depth = n // 2
    real_rows = token_total * slot_count
    capacity = round_up(real_rows * 3 // (2 * experts), 2 * row_align)
    block = capacity
    half_tokens = token_total // 2
    swap = [(0, 1), (1, 0)]
    rows = round_up(real_rows + row_align * experts, max(n * row_align, row_unit))
    chunk = rows // n
    all_rows = rows + capacity
    bf16 = jnp.bfloat16

    place, table = routing_tables(expert_ids, experts)
    peer_tokens = lax.ppermute(tokens, "hid", swap)
    shift = lax.axis_index("hid") * half_tokens
    own_place = lax.dynamic_slice_in_dim(place, shift, half_tokens)
    peer_place = lax.dynamic_slice_in_dim(place, half_tokens - shift, half_tokens)
    own_scale = lax.dynamic_slice_in_dim(gate_scale, shift, half_tokens)
    peer_scale = lax.dynamic_slice_in_dim(gate_scale, half_tokens - shift, half_tokens)
    local_place = jnp.concatenate([own_place, peer_place]).T

    partial = pl.pallas_call(
        functools.partial(up_kernel, experts, real_rows, rows, chunk, block),
        out_shape=jax.ShapeDtypeStruct((slices, all_rows, 2 * lane_width), bf16),
        grid_spec=pltpu.PrefetchScalarGridSpec(
            num_scalar_prefetch=1,
            grid=(experts,),
            in_specs=[
                whole_block((slot_count, token_total)),
                whole_block((half_tokens, width)),
                whole_block((half_tokens, width)),
                pl.BlockSpec((1, width, half_hidden), lambda e, table: (e, 0, 0)),
                pl.BlockSpec((1, width, half_hidden), lambda e, table: (e, 0, 0)),
            ],
            out_specs=whole_block((slices, all_rows, 2 * lane_width)),
            scratch_shapes=[pltpu.VMEM((all_rows, width), bf16)],
        ),
        compiler_params=pltpu.CompilerParams(vmem_limit_bytes=vmem_bytes),
    )(table, local_place, tokens, peer_tokens, gate_weight, up_weight)

    dma = pltpu.SemaphoreType.DMA
    hidden = pl.pallas_call(
        functools.partial(exchange_kernel, n, rows),
        out_shape=jax.ShapeDtypeStruct((slices, all_rows, lane_width), bf16),
        in_specs=[pl.BlockSpec(memory_space=pl.ANY)],
        out_specs=pl.BlockSpec(memory_space=pl.ANY),
        scratch_shapes=[
            pltpu.VMEM((slices, rows // 2, 2 * lane_width), bf16),
            pltpu.VMEM((slices, rows // 2, 2 * lane_width), bf16),
            pltpu.VMEM((slices, depth - 1, chunk, 2 * lane_width), bf16),
            pltpu.VMEM((slices, rows, lane_width), bf16),
            dma((slices,)),
            dma((slices, depth)),
            dma((slices, depth)),
            dma((slices, depth - 1)),
            dma((slices, depth - 1)),
            dma((slices, depth - 1)),
            dma((slices, depth - 1)),
            dma((slices, depth)),
            dma((slices, depth)),
            dma((slices,)),
        ],
        compiler_params=pltpu.CompilerParams(
            collective_id=0, has_side_effects=True, vmem_limit_bytes=vmem_bytes
        ),
    )(partial)

    peer_sum, held = pl.pallas_call(
        functools.partial(down_kernel, experts, real_rows, rows, block),
        out_shape=[
            jax.ShapeDtypeStruct((half_tokens, width), bf16),
            jax.ShapeDtypeStruct((all_rows, width), bf16),
        ],
        grid_spec=pltpu.PrefetchScalarGridSpec(
            num_scalar_prefetch=1,
            grid=(experts,),
            in_specs=[
                whole_block((half_tokens, slot_count)),
                whole_block((half_tokens, slot_count)),
                whole_block((slices, all_rows, lane_width)),
                pl.BlockSpec((1, half_hidden, width), lambda e, table: (e, 0, 0)),
            ],
            out_specs=[whole_block((half_tokens, width)), whole_block((all_rows, width))],
        ),
        compiler_params=pltpu.CompilerParams(vmem_limit_bytes=vmem_bytes),
    )(table, peer_place, peer_scale, hidden, down_weight)
    received = lax.ppermute(peer_sum, "hid", swap)
    own_sum = pl.pallas_call(
        functools.partial(own_kernel, rows),
        out_shape=jax.ShapeDtypeStruct((half_tokens, width), jnp.float32),
        in_specs=[pl.BlockSpec(memory_space=pltpu.VMEM)] * 3,
        out_specs=pl.BlockSpec(memory_space=pltpu.VMEM),
        compiler_params=pltpu.CompilerParams(vmem_limit_bytes=vmem_bytes),
        cost_estimate=pl.CostEstimate(
            flops=2 * half_tokens * rows * width,
            bytes_accessed=2 * all_rows * width,
            transcendentals=0,
        ),
    )(own_place, own_scale, held)
    return (own_sum + received.astype(jnp.float32)).astype(bf16)


def solution(mesh):
    placed = (
        P(("groups", "hid"), "wide"),
        P("groups", None),
        P("groups", None),
        P(None, "wide", "hid"),
        P(None, "wide", "hid"),
        P(None, "hid", "wide"),
    )
    return jax.shard_map(
        functools.partial(body, mesh.shape["wide"]),
        mesh=mesh,
        in_specs=placed,
        out_specs=P(("groups", "hid"), "wide"),
        check_vma=False,
    )
```

```python
import functools

import jax
import jax.numpy as jnp
from jax import lax
from jax.experimental import pallas as pl
from jax.experimental.pallas import tpu as pltpu
from jax.sharding import PartitionSpec as P

row_align = 16
lane_width = 128
row_unit = 256
combine_step = 512
y_window = 3
vmem_bytes = 60 * 1024 * 1024


def round_up(value, unit):
    return (value + unit - 1) // unit * unit


def routing_tables(expert_ids, experts):
    flat_ids = expert_ids.reshape(-1)
    labels = jnp.arange(experts, dtype=jnp.int32)
    onehot = (labels[:, None] == flat_ids[None, :]).astype(jnp.int32)
    running = jnp.cumsum(onehot, axis=1)
    counts = running[:, -1]
    padded = (counts + row_align - 1) // row_align * row_align
    starts = jnp.sum(jnp.where(labels[None, :] < labels[:, None], padded[None, :], 0), axis=1)
    place = jnp.sum(onehot * (running - 1 + starts[:, None]), axis=0)
    return place.reshape(expert_ids.shape), jnp.concatenate([starts, counts]).astype(jnp.int32)


def up_kernel(experts, real_rows, rows, step_rows, block, table, place, mine, peer, gate, up, out, gathered):
    expert = pl.program_id(0)
    half = mine.shape[0]

    @pl.when(expert == 0)
    def _():
        tail = gathered.shape[0] - rows
        gathered[rows:, :] = jnp.zeros((tail, gathered.shape[1]), gathered.dtype)
        rest = out.shape[1] - real_rows
        out[:, real_rows:, :] = jnp.zeros((out.shape[0], rest, out.shape[2]), out.dtype)
        first, second = place[0:1, :], place[1:2, :]

        def gather(step, carry):
            base = pl.multiple_of(step * step_rows, row_align)
            ids = lax.broadcasted_iota(jnp.int32, (step_rows, 2 * half), 0) + base
            chosen = jnp.where((ids == first) | (ids == second), 1.0, 0.0).astype(jnp.bfloat16)
            picked = jnp.dot(chosen[:, :half], mine[...], preferred_element_type=jnp.float32)
            picked += jnp.dot(chosen[:, half:], peer[...], preferred_element_type=jnp.float32)
            gathered[pl.ds(base, step_rows), :] = picked.astype(jnp.bfloat16)
            return carry

        lax.fori_loop(0, rows // step_rows, gather, 0)

    base = pl.multiple_of(table[expert], row_align)
    part = gathered[pl.ds(base, block), :]
    gates = jnp.dot(part, gate[0], preferred_element_type=jnp.float32).astype(jnp.bfloat16)
    ups = jnp.dot(part, up[0], preferred_element_type=jnp.float32).astype(jnp.bfloat16)
    for s in range(out.shape[0]):
        cut = slice(s * lane_width, (s + 1) * lane_width)
        out[s, pl.ds(base, block), 0:lane_width] = gates[:, cut]
        out[s, pl.ds(base, block), lane_width:] = ups[:, cut]


def exchange_kernel(n, rows, partial, result, own, paired, summed, hidden, *sems):
    own_sem, y_send, y_recv, z_send, z_recv, g_send, g_recv, h_send, h_recv, out_sem = sems
    slices = own.shape[0]
    depth = n // 2
    chunk = rows // n
    half = rows // 2
    me = lax.axis_index("wide")
    y, z = lax.rem(me, 2), lax.div(me, 2)
    y_peer = {"wide": me + 1 - 2 * y}
    ahead = [{"wide": lax.rem(z + j, depth) * 2 + y} for j in range(depth)]
    mesh_type = pl.DeviceIdType.MESH

    def span(base, j):
        return pl.ds(pl.multiple_of(base + lax.rem(z + j, depth) * chunk, row_align), chunk)

    own_base = y * half
    peer_base = (1 - y) * half

    def own_copy(s):
        return pltpu.make_async_copy(
            partial.at[s, pl.ds(pl.multiple_of(own_base, row_align), half)],
            own.at[s], own_sem.at[s],
        )

    def y_copy(s, j):
        return pltpu.make_async_remote_copy(
            partial.at[s, span(peer_base, j)], paired.at[s, span(0, j)],
            y_send.at[s, j], y_recv.at[s, j], y_peer, mesh_type,
        )

    def z_copy(s, j):
        return pltpu.make_async_remote_copy(
            own.at[s, span(0, j)], summed.at[s, j - 1],
            z_send.at[s, j - 1], z_recv.at[s, j - 1], ahead[j], mesh_type,
        )

    def chunk_of(base, index):
        return pl.ds(pl.multiple_of(base + index * chunk, row_align), chunk)

    def g_copy(s, side, hop):
        source = z - hop + 1 if side == 0 else z + hop - 1
        target = me + 2 if side == 0 else me - 2
        rows_of = chunk_of(own_base, source)
        return pltpu.make_async_remote_copy(
            hidden.at[s, rows_of], hidden.at[s, rows_of],
            g_send.at[s, side * depth + hop], g_recv.at[s, side * depth + hop],
            {"wide": target}, mesh_type,
        )

    def sends(side, hop):
        if side == 0:
            return jnp.logical_and(z < depth - 1, z - hop + 1 >= 0)
        return jnp.logical_and(z > 0, z + hop - 1 < depth)

    def g_start(s, side, hop):
        @pl.when(sends(side, hop))
        def _():
            g_copy(s, side, hop).start()

    def receives(side, hop):
        return z - hop >= 0 if side == 0 else z + hop < depth

    def arrived(side, hop):
        return chunk_of(own_base, z - hop if side == 0 else z + hop)

    def g_wait(s, side, hop):
        rows_of = arrived(side, hop)
        pltpu.make_async_remote_copy(
            hidden.at[s, rows_of], hidden.at[s, rows_of],
            g_send.at[s, side * depth + hop], g_recv.at[s, side * depth + hop],
            y_peer, mesh_type,
        ).wait_recv()

    def h_copy(s, side, hop):
        rows_of = arrived(side, hop)
        return pltpu.make_async_remote_copy(
            hidden.at[s, rows_of], hidden.at[s, rows_of],
            h_send.at[s, side * depth + hop], h_recv.at[s, side * depth + hop],
            y_peer, mesh_type,
        )

    def out_copy(s):
        return pltpu.make_async_copy(
            hidden.at[s], result.at[s, pl.ds(0, rows)], out_sem.at[s]
        )

    barrier = pltpu.get_barrier_semaphore()
    for peer in [y_peer] + ahead[1:]:
        pl.semaphore_signal(barrier, inc=1, device_id=peer, device_id_type=mesh_type)
    for s in range(slices):
        own_copy(s).start()
    pl.semaphore_wait(barrier, depth)
    far_first = sorted(range(1, depth), key=lambda j: -min(j, depth - j))
    near_first = far_first[::-1]
    pieces = [(s, j) for s in range(slices) for j in far_first + [0]]
    for s, j in pieces[:y_window]:
        y_copy(s, j).start()

    def reduce(s):
        total = own[s, span(0, 0)].astype(jnp.float32)
        for j in near_first:
            z_copy(s, j).wait_recv()
        for j in near_first:
            total = total + summed[s, j - 1].astype(jnp.float32)
        gates, ups = total[:, :lane_width], total[:, lane_width:]
        hidden[s, span(own_base, 0)] = (gates / (1.0 + jnp.exp(-gates)) * ups).astype(jnp.bfloat16)
        for side in (0, 1):
            g_start(s, side, 1)
        h_copy(s, 0, 0).start()

    def forward(s, hop):
        for side in (0, 1):
            @pl.when(receives(side, hop))
            def _(side=side):
                g_wait(s, side, hop)
                if hop + 1 < depth:
                    g_start(s, side, hop + 1)
                h_copy(s, side, hop).start()

    def finish(s):
        h_copy(s, 0, 0).wait_recv()
        for side in (0, 1):
            for hop in range(1, depth):
                @pl.when(receives(side, hop))
                def _(side=side, hop=hop):
                    h_copy(s, side, hop).wait_recv()
        out_copy(s).start()

    for step in range(slices + 3):
        if step < slices:
            own_copy(step).wait()
            for k in range(step * depth, (step + 1) * depth):
                s, j = pieces[k]
                y_copy(s, j).wait_recv()
                if k + y_window < len(pieces):
                    y_copy(*pieces[k + y_window]).start()
                part = span(0, j)
                own[s, part] = (
                    own[s, part].astype(jnp.float32) + paired[s, part].astype(jnp.float32)
                ).astype(jnp.bfloat16)
                if j > 0:
                    z_copy(s, j).start()
                hop = k - step * depth
                if hop > 0 and step >= 2:
                    forward(step - 2, hop)
        elif step - 2 < slices:
            for hop in range(1, depth):
                forward(step - 2, hop)
        if 0 <= step - 1 < slices:
            reduce(step - 1)
        if 0 <= step - 3 < slices:
            finish(step - 3)
    for s in range(slices):
        for j in range(depth):
            y_copy(s, j).wait_send()
        h_copy(s, 0, 0).wait_send()
        for j in range(1, depth):
            z_copy(s, j).wait_send()
            for side in (0, 1):
                @pl.when(sends(side, j))
                def _(s=s, side=side, j=j):
                    g_copy(s, side, j).wait_send()

                @pl.when(receives(side, j))
                def _(s=s, side=side, j=j):
                    h_copy(s, side, j).wait_send()
        out_copy(s).wait()


def combine_rows(rows, place, scale, held, out):
    def combine(step, carry):
        span = pl.ds(pl.multiple_of(step * combine_step, combine_step), combine_step)
        ids = lax.broadcasted_iota(jnp.int32, (combine_step, rows), 1)
        places, scales = place[span, :], scale[span, :]
        mixed = jnp.where(
            ids == places[:, 0:1], scales[:, 0:1],
            jnp.where(ids == places[:, 1:2], scales[:, 1:2], 0.0),
        ).astype(jnp.bfloat16)
        total = jnp.dot(mixed, held[0:rows, :], preferred_element_type=jnp.float32)
        out[span, :] = total.astype(out.dtype)
        return carry

    lax.fori_loop(0, out.shape[0] // combine_step, combine, 0)


def down_kernel(experts, real_rows, rows, block, table, place, scale, hidden, weight, out, held):
    expert = pl.program_id(0)

    @pl.when(expert == 0)
    def _():
        rest = held.shape[0] - real_rows
        held[real_rows:, :] = jnp.zeros((rest, held.shape[1]), held.dtype)

    base = pl.multiple_of(table[expert], row_align)
    part = jnp.concatenate(
        [hidden[s, pl.ds(base, block), :] for s in range(hidden.shape[0])], axis=1
    )
    product = jnp.dot(part, weight[0], preferred_element_type=jnp.float32)
    held[pl.ds(base, block), :] = product.astype(jnp.bfloat16)

    @pl.when(expert == experts - 1)
    def _():
        combine_rows(rows, place, scale, held, out)


def own_kernel(rows, place, scale, held, out):
    combine_rows(rows, place, scale, held, out)


def whole_block(shape):
    return pl.BlockSpec(
        shape, lambda e, table: (0,) * len(shape), pipeline_mode=pl.Buffered(1)
    )


def body(n, tokens, expert_ids, gate_scale, gate_weight, up_weight, down_weight):
    token_total, slot_count = expert_ids.shape
    experts, width, half_hidden = gate_weight.shape
    slices = half_hidden // lane_width
    depth = n // 2
    real_rows = token_total * slot_count
    capacity = round_up(real_rows * 3 // (2 * experts), 2 * row_align)
    block = capacity
    half_tokens = token_total // 2
    swap = [(0, 1), (1, 0)]
    rows = round_up(real_rows + row_align * experts, max(n * row_align, row_unit))
    chunk = rows // n
    all_rows = rows + capacity
    bf16 = jnp.bfloat16

    place, table = routing_tables(expert_ids, experts)
    peer_tokens = lax.ppermute(tokens, "hid", swap)
    shift = lax.axis_index("hid") * half_tokens
    own_place = lax.dynamic_slice_in_dim(place, shift, half_tokens)
    peer_place = lax.dynamic_slice_in_dim(place, half_tokens - shift, half_tokens)
    own_scale = lax.dynamic_slice_in_dim(gate_scale, shift, half_tokens)
    peer_scale = lax.dynamic_slice_in_dim(gate_scale, half_tokens - shift, half_tokens)
    local_place = jnp.concatenate([own_place, peer_place]).T

    partial = pl.pallas_call(
        functools.partial(up_kernel, experts, real_rows, rows, chunk, block),
        out_shape=jax.ShapeDtypeStruct((slices, all_rows, 2 * lane_width), bf16),
        grid_spec=pltpu.PrefetchScalarGridSpec(
            num_scalar_prefetch=1,
            grid=(experts,),
            in_specs=[
                whole_block((slot_count, token_total)),
                whole_block((half_tokens, width)),
                whole_block((half_tokens, width)),
                pl.BlockSpec((1, width, half_hidden), lambda e, table: (e, 0, 0)),
                pl.BlockSpec((1, width, half_hidden), lambda e, table: (e, 0, 0)),
            ],
            out_specs=whole_block((slices, all_rows, 2 * lane_width)),
            scratch_shapes=[pltpu.VMEM((all_rows, width), bf16)],
        ),
        compiler_params=pltpu.CompilerParams(vmem_limit_bytes=vmem_bytes),
    )(table, local_place, tokens, peer_tokens, gate_weight, up_weight)

    dma = pltpu.SemaphoreType.DMA
    hidden = pl.pallas_call(
        functools.partial(exchange_kernel, n, rows),
        out_shape=jax.ShapeDtypeStruct((slices, all_rows, lane_width), bf16),
        in_specs=[pl.BlockSpec(memory_space=pl.ANY)],
        out_specs=pl.BlockSpec(memory_space=pl.ANY),
        scratch_shapes=[
            pltpu.VMEM((slices, rows // 2, 2 * lane_width), bf16),
            pltpu.VMEM((slices, rows // 2, 2 * lane_width), bf16),
            pltpu.VMEM((slices, depth - 1, chunk, 2 * lane_width), bf16),
            pltpu.VMEM((slices, rows, lane_width), bf16),
            dma((slices,)),
            dma((slices, depth)),
            dma((slices, depth)),
            dma((slices, depth - 1)),
            dma((slices, depth - 1)),
            dma((slices, 2 * depth)),
            dma((slices, 2 * depth)),
            dma((slices, 2 * depth)),
            dma((slices, 2 * depth)),
            dma((slices,)),
        ],
        compiler_params=pltpu.CompilerParams(
            collective_id=0, has_side_effects=True, vmem_limit_bytes=vmem_bytes
        ),
    )(partial)

    peer_sum, held = pl.pallas_call(
        functools.partial(down_kernel, experts, real_rows, rows, block),
        out_shape=[
            jax.ShapeDtypeStruct((half_tokens, width), bf16),
            jax.ShapeDtypeStruct((all_rows, width), bf16),
        ],
        grid_spec=pltpu.PrefetchScalarGridSpec(
            num_scalar_prefetch=1,
            grid=(experts,),
            in_specs=[
                whole_block((half_tokens, slot_count)),
                whole_block((half_tokens, slot_count)),
                whole_block((slices, all_rows, lane_width)),
                pl.BlockSpec((1, half_hidden, width), lambda e, table: (e, 0, 0)),
            ],
            out_specs=[whole_block((half_tokens, width)), whole_block((all_rows, width))],
        ),
        compiler_params=pltpu.CompilerParams(vmem_limit_bytes=vmem_bytes),
    )(table, peer_place, peer_scale, hidden, down_weight)
    received = lax.ppermute(peer_sum, "hid", swap)
    own_sum = pl.pallas_call(
        functools.partial(own_kernel, rows),
        out_shape=jax.ShapeDtypeStruct((half_tokens, width), jnp.float32),
        in_specs=[pl.BlockSpec(memory_space=pltpu.VMEM)] * 3,
        out_specs=pl.BlockSpec(memory_space=pltpu.VMEM),
        compiler_params=pltpu.CompilerParams(vmem_limit_bytes=vmem_bytes),
        cost_estimate=pl.CostEstimate(
            flops=2 * half_tokens * rows * width,
            bytes_accessed=2 * all_rows * width,
            transcendentals=0,
        ),
    )(own_place, own_scale, held)
    return (own_sum + received.astype(jnp.float32)).astype(bf16)


def solution(mesh):
    placed = (
        P(("groups", "hid"), "wide"),
        P("groups", None),
        P("groups", None),
        P(None, "wide", "hid"),
        P(None, "wide", "hid"),
        P(None, "hid", "wide"),
    )
    return jax.shard_map(
        functools.partial(body, mesh.shape["wide"]),
        mesh=mesh,
        in_specs=placed,
        out_specs=P(("groups", "hid"), "wide"),
        check_vma=False,
    )
```

```python
import functools

import jax
import jax.numpy as jnp
from jax import lax
from jax.experimental import pallas as pl
from jax.experimental.pallas import tpu as pltpu
from jax.sharding import PartitionSpec as P

row_align = 16
lane_width = 128
row_unit = 256
combine_step = 512
y_window = 3
vmem_bytes = 60 * 1024 * 1024


def round_up(value, unit):
    return (value + unit - 1) // unit * unit


def routing_tables(expert_ids, experts):
    flat_ids = expert_ids.reshape(-1)
    labels = jnp.arange(experts, dtype=jnp.int32)
    onehot = (labels[:, None] == flat_ids[None, :]).astype(jnp.int32)
    blocks = onehot.reshape(experts, -1, lane_width).astype(jnp.bfloat16)
    within = jnp.einsum(
        "ebi,ij->ebj", blocks, jnp.triu(jnp.ones((lane_width, lane_width), jnp.bfloat16)),
        preferred_element_type=jnp.float32,
    )
    block_total = blocks.shape[1]
    before = jnp.einsum(
        "eb,bc->ec", within[:, :, -1].astype(jnp.bfloat16),
        jnp.triu(jnp.ones((block_total, block_total), jnp.bfloat16), 1),
        preferred_element_type=jnp.float32,
    )
    running = (within + before[:, :, None]).reshape(experts, -1).astype(jnp.int32)
    counts = running[:, -1]
    padded = (counts + row_align - 1) // row_align * row_align
    starts = jnp.sum(jnp.where(labels[None, :] < labels[:, None], padded[None, :], 0), axis=1)
    place = jnp.sum(onehot * (running - 1 + starts[:, None]), axis=0)
    return place.reshape(expert_ids.shape), jnp.concatenate([starts, counts]).astype(jnp.int32)


def up_kernel(experts, real_rows, rows, step_rows, block, table, place, mine, peer, gate, up, out, gathered):
    expert = pl.program_id(0)
    half = mine.shape[0]

    @pl.when(expert == 0)
    def _():
        tail = gathered.shape[0] - rows
        gathered[rows:, :] = jnp.zeros((tail, gathered.shape[1]), gathered.dtype)
        rest = out.shape[1] - real_rows
        out[:, real_rows:, :] = jnp.zeros((out.shape[0], rest, out.shape[2]), out.dtype)
        first, second = place[0:1, :], place[1:2, :]

        def gather(step, carry):
            base = pl.multiple_of(step * step_rows, row_align)
            ids = lax.broadcasted_iota(jnp.int32, (step_rows, 2 * half), 0) + base
            chosen = jnp.where((ids == first) | (ids == second), 1.0, 0.0).astype(jnp.bfloat16)
            picked = jnp.dot(chosen[:, :half], mine[...], preferred_element_type=jnp.float32)
            picked += jnp.dot(chosen[:, half:], peer[...], preferred_element_type=jnp.float32)
            gathered[pl.ds(base, step_rows), :] = picked.astype(jnp.bfloat16)
            return carry

        lax.fori_loop(0, rows // step_rows, gather, 0)

    base = pl.multiple_of(table[expert], row_align)
    part = gathered[pl.ds(base, block), :]
    gates = jnp.dot(part, gate[0], preferred_element_type=jnp.float32).astype(jnp.bfloat16)
    ups = jnp.dot(part, up[0], preferred_element_type=jnp.float32).astype(jnp.bfloat16)
    for s in range(out.shape[0]):
        cut = slice(s * lane_width, (s + 1) * lane_width)
        out[s, pl.ds(base, block), 0:lane_width] = gates[:, cut]
        out[s, pl.ds(base, block), lane_width:] = ups[:, cut]


def exchange_kernel(n, rows, partial, result, own, paired, summed, hidden, *sems):
    own_sem, y_send, y_recv, z_send, z_recv, g_send, g_recv, h_send, h_recv, out_sem = sems
    slices = own.shape[0]
    depth = n // 2
    chunk = rows // n
    half = rows // 2
    me = lax.axis_index("wide")
    y, z = lax.rem(me, 2), lax.div(me, 2)
    y_peer = {"wide": me + 1 - 2 * y}
    ahead = [{"wide": lax.rem(z + j, depth) * 2 + y} for j in range(depth)]
    mesh_type = pl.DeviceIdType.MESH

    def span(base, j):
        return pl.ds(pl.multiple_of(base + lax.rem(z + j, depth) * chunk, row_align), chunk)

    own_base = y * half
    peer_base = (1 - y) * half

    def own_copy(s):
        return pltpu.make_async_copy(
            partial.at[s, pl.ds(pl.multiple_of(own_base, row_align), half)],
            own.at[s], own_sem.at[s],
        )

    def y_copy(s, j):
        return pltpu.make_async_remote_copy(
            partial.at[s, span(peer_base, j)], paired.at[s, span(0, j)],
            y_send.at[s, j], y_recv.at[s, j], y_peer, mesh_type,
        )

    def z_copy(s, j):
        return pltpu.make_async_remote_copy(
            own.at[s, span(0, j)], summed.at[s, j - 1],
            z_send.at[s, j - 1], z_recv.at[s, j - 1], ahead[j], mesh_type,
        )

    def chunk_of(base, index):
        return pl.ds(pl.multiple_of(base + index * chunk, row_align), chunk)

    def g_copy(s, side, hop):
        source = z - hop + 1 if side == 0 else z + hop - 1
        target = me + 2 if side == 0 else me - 2
        rows_of = chunk_of(own_base, source)
        return pltpu.make_async_remote_copy(
            hidden.at[s, rows_of], hidden.at[s, rows_of],
            g_send.at[s, side * depth + hop], g_recv.at[s, side * depth + hop],
            {"wide": target}, mesh_type,
        )

    def sends(side, hop):
        if side == 0:
            return jnp.logical_and(z < depth - 1, z - hop + 1 >= 0)
        return jnp.logical_and(z > 0, z + hop - 1 < depth)

    def g_start(s, side, hop):
        @pl.when(sends(side, hop))
        def _():
            g_copy(s, side, hop).start()

    def receives(side, hop):
        return z - hop >= 0 if side == 0 else z + hop < depth

    def arrived(side, hop):
        return chunk_of(own_base, z - hop if side == 0 else z + hop)

    def g_wait(s, side, hop):
        rows_of = arrived(side, hop)
        pltpu.make_async_remote_copy(
            hidden.at[s, rows_of], hidden.at[s, rows_of],
            g_send.at[s, side * depth + hop], g_recv.at[s, side * depth + hop],
            y_peer, mesh_type,
        ).wait_recv()

    def h_copy(s, side, hop):
        rows_of = arrived(side, hop)
        return pltpu.make_async_remote_copy(
            hidden.at[s, rows_of], hidden.at[s, rows_of],
            h_send.at[s, side * depth + hop], h_recv.at[s, side * depth + hop],
            y_peer, mesh_type,
        )

    def out_copy(s):
        return pltpu.make_async_copy(
            hidden.at[s], result.at[s, pl.ds(0, rows)], out_sem.at[s]
        )

    barrier = pltpu.get_barrier_semaphore()
    for peer in [y_peer] + ahead[1:]:
        pl.semaphore_signal(barrier, inc=1, device_id=peer, device_id_type=mesh_type)
    for s in range(slices):
        own_copy(s).start()
    pl.semaphore_wait(barrier, depth)
    far_first = sorted(range(1, depth), key=lambda j: -min(j, depth - j))
    near_first = far_first[::-1]
    pieces = [(s, j) for s in range(slices) for j in far_first + [0]]
    for s, j in pieces[:y_window]:
        y_copy(s, j).start()

    def reduce(s):
        total = own[s, span(0, 0)].astype(jnp.float32)
        for j in near_first:
            z_copy(s, j).wait_recv()
        for j in near_first:
            total = total + summed[s, j - 1].astype(jnp.float32)
        gates, ups = total[:, :lane_width], total[:, lane_width:]
        hidden[s, span(own_base, 0)] = (gates / (1.0 + jnp.exp(-gates)) * ups).astype(jnp.bfloat16)
        for side in (0, 1):
            g_start(s, side, 1)
        h_copy(s, 0, 0).start()

    def forward(s, hop):
        for side in (0, 1):
            @pl.when(receives(side, hop))
            def _(side=side):
                g_wait(s, side, hop)
                if hop + 1 < depth:
                    g_start(s, side, hop + 1)
                h_copy(s, side, hop).start()

    def finish(s):
        h_copy(s, 0, 0).wait_recv()
        for side in (0, 1):
            for hop in range(1, depth):
                @pl.when(receives(side, hop))
                def _(side=side, hop=hop):
                    h_copy(s, side, hop).wait_recv()
        out_copy(s).start()

    for step in range(slices + 3):
        if step < slices:
            own_copy(step).wait()
            for k in range(step * depth, (step + 1) * depth):
                s, j = pieces[k]
                y_copy(s, j).wait_recv()
                if k + y_window < len(pieces):
                    y_copy(*pieces[k + y_window]).start()
                part = span(0, j)
                own[s, part] = (
                    own[s, part].astype(jnp.float32) + paired[s, part].astype(jnp.float32)
                ).astype(jnp.bfloat16)
                if j > 0:
                    z_copy(s, j).start()
                hop = k - step * depth
                if hop > 0 and step >= 2:
                    forward(step - 2, hop)
        elif step - 2 < slices:
            for hop in range(1, depth):
                forward(step - 2, hop)
        if 0 <= step - 1 < slices:
            reduce(step - 1)
        if 0 <= step - 3 < slices:
            finish(step - 3)
    for s in range(slices):
        for j in range(depth):
            y_copy(s, j).wait_send()
        h_copy(s, 0, 0).wait_send()
        for j in range(1, depth):
            z_copy(s, j).wait_send()
            for side in (0, 1):
                @pl.when(sends(side, j))
                def _(s=s, side=side, j=j):
                    g_copy(s, side, j).wait_send()

                @pl.when(receives(side, j))
                def _(s=s, side=side, j=j):
                    h_copy(s, side, j).wait_send()
        out_copy(s).wait()


def combine_rows(rows, place, scale, held, out):
    def combine(step, carry):
        span = pl.ds(pl.multiple_of(step * combine_step, combine_step), combine_step)
        ids = lax.broadcasted_iota(jnp.int32, (combine_step, rows), 1)
        places, scales = place[span, :], scale[span, :]
        mixed = jnp.where(
            ids == places[:, 0:1], scales[:, 0:1],
            jnp.where(ids == places[:, 1:2], scales[:, 1:2], 0.0),
        ).astype(jnp.bfloat16)
        total = jnp.dot(mixed, held[0:rows, :], preferred_element_type=jnp.float32)
        out[span, :] = total.astype(out.dtype)
        return carry

    lax.fori_loop(0, out.shape[0] // combine_step, combine, 0)


def down_kernel(experts, real_rows, rows, block, table, place, scale, hidden, weight, out, held):
    expert = pl.program_id(0)

    @pl.when(expert == 0)
    def _():
        rest = held.shape[0] - real_rows
        held[real_rows:, :] = jnp.zeros((rest, held.shape[1]), held.dtype)

    base = pl.multiple_of(table[expert], row_align)
    part = jnp.concatenate(
        [hidden[s, pl.ds(base, block), :] for s in range(hidden.shape[0])], axis=1
    )
    product = jnp.dot(part, weight[0], preferred_element_type=jnp.float32)
    held[pl.ds(base, block), :] = product.astype(jnp.bfloat16)

    @pl.when(expert == experts - 1)
    def _():
        combine_rows(rows, place, scale, held, out)


def own_kernel(rows, place, scale, held, out):
    combine_rows(rows, place, scale, held, out)


def whole_block(shape):
    return pl.BlockSpec(
        shape, lambda e, table: (0,) * len(shape), pipeline_mode=pl.Buffered(1)
    )


def body(n, tokens, expert_ids, gate_scale, gate_weight, up_weight, down_weight):
    token_total, slot_count = expert_ids.shape
    experts, width, half_hidden = gate_weight.shape
    slices = half_hidden // lane_width
    depth = n // 2
    real_rows = token_total * slot_count
    capacity = round_up(real_rows * 3 // (2 * experts), 2 * row_align)
    block = capacity
    half_tokens = token_total // 2
    swap = [(0, 1), (1, 0)]
    rows = round_up(real_rows + row_align * experts, max(n * row_align, row_unit))
    chunk = rows // n
    all_rows = rows + capacity
    bf16 = jnp.bfloat16

    place, table = routing_tables(expert_ids, experts)
    peer_tokens = lax.ppermute(tokens, "hid", swap)
    shift = lax.axis_index("hid") * half_tokens
    own_place = lax.dynamic_slice_in_dim(place, shift, half_tokens)
    peer_place = lax.dynamic_slice_in_dim(place, half_tokens - shift, half_tokens)
    own_scale = lax.dynamic_slice_in_dim(gate_scale, shift, half_tokens)
    peer_scale = lax.dynamic_slice_in_dim(gate_scale, half_tokens - shift, half_tokens)
    local_place = jnp.concatenate([own_place, peer_place]).T

    partial = pl.pallas_call(
        functools.partial(up_kernel, experts, real_rows, rows, chunk, block),
        out_shape=jax.ShapeDtypeStruct((slices, all_rows, 2 * lane_width), bf16),
        grid_spec=pltpu.PrefetchScalarGridSpec(
            num_scalar_prefetch=1,
            grid=(experts,),
            in_specs=[
                whole_block((slot_count, token_total)),
                whole_block((half_tokens, width)),
                whole_block((half_tokens, width)),
                pl.BlockSpec((1, width, half_hidden), lambda e, table: (e, 0, 0)),
                pl.BlockSpec((1, width, half_hidden), lambda e, table: (e, 0, 0)),
            ],
            out_specs=whole_block((slices, all_rows, 2 * lane_width)),
            scratch_shapes=[pltpu.VMEM((all_rows, width), bf16)],
        ),
        compiler_params=pltpu.CompilerParams(vmem_limit_bytes=vmem_bytes),
    )(table, local_place, tokens, peer_tokens, gate_weight, up_weight)

    dma = pltpu.SemaphoreType.DMA
    hidden = pl.pallas_call(
        functools.partial(exchange_kernel, n, rows),
        out_shape=jax.ShapeDtypeStruct((slices, all_rows, lane_width), bf16),
        in_specs=[pl.BlockSpec(memory_space=pl.ANY)],
        out_specs=pl.BlockSpec(memory_space=pl.ANY),
        scratch_shapes=[
            pltpu.VMEM((slices, rows // 2, 2 * lane_width), bf16),
            pltpu.VMEM((slices, rows // 2, 2 * lane_width), bf16),
            pltpu.VMEM((slices, depth - 1, chunk, 2 * lane_width), bf16),
            pltpu.VMEM((slices, rows, lane_width), bf16),
            dma((slices,)),
            dma((slices, depth)),
            dma((slices, depth)),
            dma((slices, depth - 1)),
            dma((slices, depth - 1)),
            dma((slices, 2 * depth)),
            dma((slices, 2 * depth)),
            dma((slices, 2 * depth)),
            dma((slices, 2 * depth)),
            dma((slices,)),
        ],
        compiler_params=pltpu.CompilerParams(
            collective_id=0, has_side_effects=True, vmem_limit_bytes=vmem_bytes
        ),
    )(partial)

    peer_sum, held = pl.pallas_call(
        functools.partial(down_kernel, experts, real_rows, rows, block),
        out_shape=[
            jax.ShapeDtypeStruct((half_tokens, width), bf16),
            jax.ShapeDtypeStruct((all_rows, width), bf16),
        ],
        grid_spec=pltpu.PrefetchScalarGridSpec(
            num_scalar_prefetch=1,
            grid=(experts,),
            in_specs=[
                whole_block((half_tokens, slot_count)),
                whole_block((half_tokens, slot_count)),
                whole_block((slices, all_rows, lane_width)),
                pl.BlockSpec((1, half_hidden, width), lambda e, table: (e, 0, 0)),
            ],
            out_specs=[whole_block((half_tokens, width)), whole_block((all_rows, width))],
        ),
        compiler_params=pltpu.CompilerParams(vmem_limit_bytes=vmem_bytes),
    )(table, peer_place, peer_scale, hidden, down_weight)
    received = lax.ppermute(peer_sum, "hid", swap)
    own_sum = pl.pallas_call(
        functools.partial(own_kernel, rows),
        out_shape=jax.ShapeDtypeStruct((half_tokens, width), bf16),
        in_specs=[pl.BlockSpec(memory_space=pltpu.VMEM)] * 3,
        out_specs=pl.BlockSpec(memory_space=pltpu.VMEM),
        compiler_params=pltpu.CompilerParams(vmem_limit_bytes=vmem_bytes),
        cost_estimate=pl.CostEstimate(
            flops=2 * half_tokens * rows * width,
            bytes_accessed=2 * all_rows * width,
            transcendentals=0,
        ),
    )(own_place, own_scale, held)
    return (own_sum.astype(jnp.float32) + received.astype(jnp.float32)).astype(bf16)


def solution(mesh):
    placed = (
        P(("groups", "hid"), "wide"),
        P("groups", None),
        P("groups", None),
        P(None, "wide", "hid"),
        P(None, "wide", "hid"),
        P(None, "hid", "wide"),
    )
    return jax.shard_map(
        functools.partial(body, mesh.shape["wide"]),
        mesh=mesh,
        in_specs=placed,
        out_specs=P(("groups", "hid"), "wide"),
        check_vma=False,
    )
```
